32 devices in a mesh: groups: 2 (over y), blk: 8 (over z, x), shard: 2 (over core).
Axes of the slice: x: 2, y: 2, z: 4, core: 2. Of those that a mesh axis runs over, the one named last changes fastest.
Arguments:
- queries: bfloat16 [8192, 768], P(('groups', 'blk')), parts along dimension 0, may hold values from -8 to 8
- passages: bfloat16 [512, 768], P(('groups', 'blk', 'shard')), parts along dimension 0, may hold values from -8 to 8
- cand_ids: int32 [8192, 32], P(('groups', 'blk')), parts along dimension 0, may hold values from 0 to 255
Outputs:
- soft_labels: float32 [8192, 32], P(('groups', 'blk')), parts along dimension 0
The draws below stay inside these ranges and needn't reach their ends.
There are 2 independent parts, one for each index of `groups`. The reference program is written for one: setup_inputs(seed, part) draws one part's arguments, and reference() takes and returns one part's arrays. A program takes and returns all parts, laid end to end along the dimension named above; each array names one. Nothing has to cross between parts.
All inputs are finite; a program needn't handle non-finite values.
Results may differ from the reference program's by a relative error of at most 0.0003.
Values may be sent and summed in bfloat16 or wider, within the bound.
No kernel may reach another device: no remote copies, remote signals or barrier semaphores. Data moves between devices by JAX's collectives and lax.ppermute only.
A program may use at most 64 MiB of HBM per device.

```python
import math
import jax
import jax.numpy as jnp
from jax import lax

D = 768
CAND = 32
Q_DEV = 512
QUERIES = 4096
PASSAGES = 256


def shared_base(key):
    raw = jnp.clip(jax.random.normal(key, (PASSAGES, D), jnp.float32), -6.0, 6.0)
    index = jnp.arange(PASSAGES)
    strong = (index % 16 == 0)[:, None]
    base = jnp.where(strong, jnp.clip(raw * 8.0, -8.0, 8.0), raw)
    partner = jnp.roll(base, 1, axis=0) * (1.0 - 0.2 / D)
    chosen = (index % 16 == 1)[:, None]
    return jnp.where(chosen, partner, base)


def draw_passages(key, part):
    return shared_base(key).astype(jnp.bfloat16)


def drawn_rows(base):
    index = jnp.arange(QUERIES)
    within = index % Q_DEV
    order = index // Q_DEV * 4 + within
    target = 16 * order % PASSAGES
    strength = jnp.array([0.5, 0.7, 1.0, 1.5], jnp.float32)[index % 4]
    aligned = jnp.clip(base[target] * strength[:, None], -8.0, 8.0)
    return (aligned, (within < 4)[:, None])


def draw_queries(key, part):
    base = shared_base(key)
    key = jax.random.fold_in(key, 7)
    aligned, chosen = drawn_rows(base)
    drawn = jnp.clip(jax.random.normal(key, (QUERIES, D), jnp.float32), -6.0, 6.0)
    return jnp.where(chosen, aligned, drawn).astype(jnp.bfloat16)


def touch_ends(values, key, low, top_value):
    place = [jax.random.randint(jax.random.fold_in(key, axis), (), 0, length) for axis, length in enumerate(values.shape)]
    longest = values.shape.index(max(values.shape))
    beside = place[:longest] + [(place[longest] + 1) % values.shape[longest]] + place[longest + 1:]
    return values.at[tuple(place)].set(low).at[tuple(beside)].set(top_value)


def setup_inputs(seed: int = 0, part: int = 0) -> dict:
    keys = jax.random.split(jax.random.key(seed), 4)
    part_keys = jax.random.split(jax.random.fold_in(keys[3], part), 4)
    return {
        "queries": draw_queries(jax.random.fold_in(jax.random.fold_in(keys[3], part), 71), part),
        "passages": draw_passages(jax.random.fold_in(jax.random.fold_in(keys[3], part), 71), part),
        "cand_ids": touch_ends(jax.random.randint(part_keys[2], (QUERIES, CAND), 0, PASSAGES), jax.random.fold_in(part_keys[2], 1), 0, PASSAGES - 1).astype(jnp.int32),
    }


SCALE = 0.2


def reference(queries, passages, cand_ids):
    total = queries.shape[0]
    width = math.gcd(total, 1024)
    qblocks = queries.reshape(total // width, width, queries.shape[1])
    iblocks = cand_ids.reshape(total // width, width, cand_ids.shape[1])

    def one_block(pair):
        block, ids = pair
        logits = SCALE * lax.dot_general(block, passages, (((1,), (1,)), ((), ())), preferred_element_type=jnp.float32)
        top = jnp.max(logits, axis=1, keepdims=True)
        normalizer = top[:, 0] + jnp.log(jnp.sum(jnp.exp(logits - top), axis=1))
        picked = jnp.take_along_axis(logits, ids.astype(jnp.int32), axis=1)
        return picked - normalizer[:, None]

    labels = lax.map(one_block, (qblocks, iblocks))
    return labels.reshape(total, cand_ids.shape[1])
```

```python
import functools

import jax
import jax.numpy as jnp
from jax import lax
from jax.experimental import pallas as pl
from jax.experimental.pallas import tpu as pltpu
from jax.sharding import PartitionSpec as P

SCALE = 0.2
AXES = ("blk", "shard")
BLOCK = 256


def parity(value):
    return value.bit_count() & 1


def step_masks(n_blk, kind):
    bits = n_blk.bit_length() - 1
    masks = [(2 << bit) | 1 for bit in range(bits - 1, -1, -1)]
    if bits >= 2 and kind:
        masks[-1], masks[-2] = masks[-2], masks[-1]
    return masks + [1]


def kind_mask(n_blk):
    return 0b111 if n_blk >= 4 else 0


def places(masks):
    reach = {0: 0}
    for step, mask in enumerate(masks):
        reach |= {source ^ mask: place | (1 << step) for source, place in reach.items()}
    return [reach[1 << bit] for bit in range(len(masks))]


def logits_of(rows, queries):
    return SCALE * lax.dot_general(
        rows, queries, (((1,), (1,)), ((), ())), preferred_element_type=jnp.float32
    )


def picked_in(logits, ids, start, before):
    chosen = []
    for top in range(0, ids.shape[0], 8):
        local = ids[top : top + 8] - start
        chunk, row = local >> 3, local & 7
        value = before[top : top + 8]
        for c in range(logits.shape[0] // 8):
            found = jnp.take_along_axis(
                logits[c * 8 : c * 8 + 8], row, axis=0, mode="promise_in_bounds"
            )
            value = jnp.where(chunk == c, found, value)
        chosen.append(value)
    return jnp.concatenate(chosen, axis=0)


def label_kernel(rows, n_blk, q_ref, own_ref, other_ref, ids_ref, out_ref, logits_ref):
    me = lax.axis_index("blk") * 2 + lax.axis_index("shard")
    kind = jnp.int32(0)
    for bit in range(kind_mask(n_blk).bit_length()):
        kind = kind ^ ((me >> bit) & 1)
    ids = ids_ref[...]
    shift = rows.bit_length() - 1
    source = (ids >> shift) ^ me
    tables = [places(step_masks(n_blk, other)) for other in (0, 1)]
    found = []
    for table in tables:
        place = jnp.zeros_like(ids)
        for bit, added in enumerate(table):
            place = place ^ (((source >> bit) & 1) * added)
        found.append(place)
    theirs = found[0] >> (len(tables[0]) - 1)
    flips = parity(kind_mask(n_blk) & 1)
    place = jnp.where((kind ^ (theirs * flips)) == 0, found[0], found[1])
    local = (place << shift) | (ids & (rows - 1))

    half = own_ref.shape[0]
    zero = jnp.zeros(ids.shape, jnp.float32)
    if half * 2 <= BLOCK:
        first = logits_of(own_ref[...], q_ref[...])
        second = logits_of(other_ref[...], q_ref[...])
        top = jnp.maximum(
            jnp.max(first, axis=0, keepdims=True), jnp.max(second, axis=0, keepdims=True)
        )
        total = jnp.sum(jnp.exp(first - top), axis=0, keepdims=True) + jnp.sum(
            jnp.exp(second - top), axis=0, keepdims=True
        )
        picked = picked_in(second, local, half, picked_in(first, local, 0, zero))
        out_ref[...] = picked - (top + jnp.log(total))
        return

    steps = half // BLOCK

    def fill(index, top):
        at = pl.multiple_of(index * BLOCK, BLOCK)
        first = logits_of(own_ref[pl.ds(at, BLOCK)], q_ref[...])
        second = logits_of(other_ref[pl.ds(at, BLOCK)], q_ref[...])
        logits_ref[pl.ds(at, BLOCK)] = first
        logits_ref[pl.ds(pl.multiple_of(half + at, BLOCK), BLOCK)] = second
        return jnp.maximum(
            top,
            jnp.maximum(
                jnp.max(first, axis=0, keepdims=True), jnp.max(second, axis=0, keepdims=True)
            ),
        )

    top = lax.fori_loop(0, steps, fill, jnp.full((1, ids.shape[1]), -jnp.inf, jnp.float32))

    def read(index, carry):
        total, picked = carry
        at = pl.multiple_of(index * BLOCK, BLOCK)
        block = logits_ref[pl.ds(at, BLOCK)]
        total = total + jnp.sum(jnp.exp(block - top), axis=0, keepdims=True)
        return (total, picked_in(block, local, at, picked))

    total, picked = lax.fori_loop(0, 2 * steps, read, (jnp.zeros_like(top), zero))
    out_ref[...] = picked - (top + jnp.log(total))


def body(queries, passages, cand_ids):
    rows = passages.shape[0]
    n_blk = lax.axis_size("blk")
    n_all = 2 * n_blk
    mix = kind_mask(n_blk)
    tables = [step_masks(n_blk, kind) for kind in (0, 1)]
    held = passages
    for step in range(len(tables[0]) - 1):
        pairs = [(i, i ^ tables[parity(i & mix)][step]) for i in range(n_all)]
        if step == 0:
            twice = lax.optimization_barrier(jnp.concatenate([held, held], axis=0))
            held = twice.at[rows:].set(lax.ppermute(held, AXES, pairs))
        else:
            held = jnp.concatenate([held, lax.ppermute(held, AXES, pairs)], axis=0)
    other = lax.ppermute(held, "shard", [(0, 1), (1, 0)])
    half = held.shape[0]
    spare = 8 if half * 2 <= BLOCK else 2 * half
    out = pl.pallas_call(
        functools.partial(label_kernel, rows, n_blk),
        out_shape=jax.ShapeDtypeStruct(cand_ids.shape[::-1], jnp.float32),
        in_specs=[pl.BlockSpec(memory_space=pltpu.VMEM)] * 4,
        out_specs=pl.BlockSpec(memory_space=pltpu.VMEM),
        scratch_shapes=[pltpu.VMEM((spare, queries.shape[0]), jnp.float32)],
        compiler_params=pltpu.CompilerParams(vmem_limit_bytes=40 * 2**20),
    )(queries, held, other, cand_ids.T)
    return out.T


def solution(mesh):
    return jax.shard_map(
        body,
        mesh=mesh,
        in_specs=(
            P(("groups", "blk"), None),
            P(("groups", "blk", "shard"), None),
            P(("groups", "blk"), None),
        ),
        out_specs=P(("groups", "blk"), None),
        check_vma=False,
    )
```

```python
import functools

import jax
import jax.numpy as jnp
from jax import lax
from jax.experimental import pallas as pl
from jax.experimental.pallas import tpu as pltpu
from jax.sharding import PartitionSpec as P

SCALE = 0.2
AXES = ("blk", "shard")
BLOCK = 256
VMEM = pl.BlockSpec(memory_space=pltpu.VMEM)


def parity(value):
    return value.bit_count() & 1


def doubling_masks(n_blk):
    return [(2 << bit) | 1 for bit in range(n_blk.bit_length() - 2, 1, -1)]


def direct_masks(kind):
    return (7, 5, 3) if kind else (7, 3, 5)


def local_ids(ids, rows, n_blk):
    me = lax.axis_index("blk") * 2 + lax.axis_index("shard")
    kind = (me ^ (me >> 1) ^ (me >> 2)) & 1
    shift = rows.bit_length() - 1
    source = (ids >> shift) ^ me
    one, two = (source >> 1) & 1, (source >> 2) & 1
    low = jnp.where(kind == 0, one, two)
    high = jnp.where(kind == 0, two, one)
    theirs = (source & 1) ^ (one | two)
    steps = doubling_masks(n_blk)
    place = ((low ^ high) << 1 | high) << len(steps)
    for step, mask in enumerate(steps):
        bit = (source >> (mask.bit_length() - 1)) & 1
        theirs = theirs ^ bit
        place = place | bit << step
    place = place | theirs << (len(steps) + 2)
    return (place << shift) | (ids & (rows - 1))


def absorb(state, logits, ids, start):
    top, total, picked = state
    new_top = jnp.maximum(top, jnp.max(logits, axis=0, keepdims=True))
    new_total = total * jnp.exp(top - new_top) + jnp.sum(
        jnp.exp(logits - new_top), axis=0, keepdims=True
    )
    chosen = []
    for k in range(0, ids.shape[0], 8):
        local = ids[k : k + 8] - start
        chunk, row = local >> 3, local & 7
        value = picked[k : k + 8]
        for c in range(logits.shape[0] // 8):
            found = jnp.take_along_axis(
                logits[c * 8 : c * 8 + 8], row, axis=0, mode="promise_in_bounds"
            )
            value = jnp.where(chunk == c, found, value)
        chosen.append(value)
    return (new_top, new_total, jnp.concatenate(chosen, axis=0))


def absorb_rows(state, refs, q_ref, ids, start):
    def one(state, rows, at):
        logits = SCALE * lax.dot_general(
            rows, q_ref[...], (((1,), (1,)), ((), ())), preferred_element_type=jnp.float32
        )
        return absorb(state, logits, ids, at)

    count = refs[0].shape[0]
    if count * len(refs) <= BLOCK:
        return one(state, jnp.concatenate([ref[...] for ref in refs], axis=0), start)

    for ref in refs:

        def step(index, state, ref=ref, start=start):
            at = pl.multiple_of(index * BLOCK, BLOCK)
            return one(state, ref[pl.ds(at, BLOCK)], start + at)

        state = lax.fori_loop(0, count // BLOCK, step, state)
        start = start + count
    return state


def empty(ids):
    wide = (1, ids.shape[1])
    return (
        jnp.full(wide, -jnp.inf, jnp.float32),
        jnp.zeros(wide, jnp.float32),
        jnp.zeros(ids.shape, jnp.float32),
    )


def first_kernel(rows, n_blk, q_ref, a_ref, b_ref, ids_ref, local_ref, top_ref, total_ref, picked_ref):
    local = local_ids(ids_ref[...], rows, n_blk)
    local_ref[...] = local
    state = absorb_rows(empty(local), (a_ref, b_ref), q_ref, local, 0)
    top_ref[...], total_ref[...], picked_ref[...] = state


def second_kernel(start, q_ref, a_ref, b_ref, local_ref, top_ref, total_ref, picked_ref, out_ref):
    state = (top_ref[...], total_ref[...], picked_ref[...])
    top, total, picked = absorb_rows(state, (a_ref, b_ref), q_ref, local_ref[...], start)
    count = picked.shape[0]
    out_ref[:count] = picked
    out_ref[count:] = jnp.broadcast_to(top + jnp.log(total), (8, picked.shape[1]))


def last_kernel(mine_ref, other_ref, out_ref):
    count = out_ref.shape[0]
    mine, other = mine_ref[count : count + 1], other_ref[count : count + 1]
    top = jnp.maximum(mine, other)
    normalizer = top + jnp.log(jnp.exp(mine - top) + jnp.exp(other - top))
    out_ref[...] = mine_ref[:count] + other_ref[:count] - normalizer


def cost(n_rows, queries, ids):
    return pl.CostEstimate(
        flops=2 * n_rows * queries.shape[0] * queries.shape[1],
        bytes_accessed=2 * (queries.size + n_rows * queries.shape[1]) + 8 * ids.size,
        transcendentals=n_rows * queries.shape[0],
    )


PARAMS = pltpu.CompilerParams(vmem_limit_bytes=40 * 2**20)


def first_call(rows, n_blk, queries, pieces, ids):
    wide = jax.ShapeDtypeStruct((1, ids.shape[1]), jnp.float32)
    return pl.pallas_call(
        functools.partial(first_kernel, rows, n_blk),
        out_shape=(
            jax.ShapeDtypeStruct(ids.shape, jnp.int32),
            wide,
            wide,
            jax.ShapeDtypeStruct(ids.shape, jnp.float32),
        ),
        in_specs=[VMEM] * 4,
        out_specs=(VMEM,) * 4,
        compiler_params=PARAMS,
        cost_estimate=cost(2 * pieces[0].shape[0], queries, ids),
    )(queries, *pieces, ids)


def second_call(queries, pieces, local, state):
    return pl.pallas_call(
        functools.partial(second_kernel, 2 * pieces[0].shape[0]),
        out_shape=jax.ShapeDtypeStruct((local.shape[0] + 8, local.shape[1]), jnp.float32),
        in_specs=[VMEM] * 7,
        out_specs=VMEM,
        compiler_params=PARAMS,
        cost_estimate=cost(2 * pieces[0].shape[0], queries, local),
    )(queries, *pieces, local, *state)


def last_call(mine, other, count):
    return pl.pallas_call(
        last_kernel,
        out_shape=jax.ShapeDtypeStruct((count, mine.shape[1]), jnp.float32),
        in_specs=[VMEM] * 2,
        out_specs=VMEM,
        compiler_params=PARAMS,
    )(mine, other)


def body(queries, passages, cand_ids):
    rows = passages.shape[0]
    n_blk = lax.axis_size("blk")
    n_all = 2 * n_blk
    direct = [direct_masks(i.bit_count() & 1) for i in range(8)]
    held = passages
    for step, mask in enumerate(doubling_masks(n_blk)):
        got = lax.ppermute(held, AXES, [(i, i ^ mask) for i in range(n_all)])
        if step == 0:
            twice = lax.optimization_barrier(jnp.concatenate([held, held], axis=0))
            held = twice.at[rows:].set(got)
        else:
            held = jnp.concatenate([held, got], axis=0)
    far, near, last = (
        lax.ppermute(held, AXES, [(i, i ^ direct[i % 8][turn]) for i in range(n_all)])
        for turn in range(3)
    )
    local, *state = first_call(rows, n_blk, queries, [held, far], cand_ids.T)
    mine = second_call(queries, [near, last], local, state)
    other = lax.ppermute(mine, "shard", [(0, 1), (1, 0)])
    return last_call(mine, other, cand_ids.shape[1]).T


def solution(mesh):
    return jax.shard_map(
        body,
        mesh=mesh,
        in_specs=(
            P(("groups", "blk"), None),
            P(("groups", "blk", "shard"), None),
            P(("groups", "blk"), None),
        ),
        out_specs=P(("groups", "blk"), None),
        check_vma=False,
    )
```

```python
import functools

import jax
import jax.numpy as jnp
from jax import lax
from jax.experimental import pallas as pl
from jax.experimental.pallas import tpu as pltpu
from jax.sharding import PartitionSpec as P

SCALE = 0.2
AXES = ("blk", "shard")
BLOCK = 256
VMEM = pl.BlockSpec(memory_space=pltpu.VMEM)


def parity(value):
    return value.bit_count() & 1


CROSSED = 0
MASKS = (3, 4, 7)
ORDERS = (
    (2, 1, 0),
    (0, 2, 1),
    (2, 0, 1),
    (2, 1, 0),
    (2, 1, 0),
    (0, 2, 1),
    (2, 0, 1),
    (2, 1, 0),
    (2, 1, 0),
    (0, 2, 1),
    (2, 0, 1),
    (2, 1, 0),
    (2, 1, 0),
    (0, 2, 1),
    (2, 0, 1),
    (2, 1, 0),
)


def doubling_masks(n_blk):
    return [(2 << bit) | CROSSED for bit in range(n_blk.bit_length() - 2, 1, -1)]


def target(number, turn):
    return number ^ MASKS[ORDERS[number & 15][turn]]


def turns_of(which):
    code = 0
    for number in range(16):
        source = number ^ MASKS[which]
        code |= ORDERS[source].index(which) << (2 * number)
    return code


def local_ids(ids, rows, n_blk):
    me = lax.axis_index("blk") * 2 + lax.axis_index("shard")
    shift = rows.bit_length() - 1
    source = (ids >> shift) ^ me
    one, two = (source >> 1) & 1, (source >> 2) & 1
    at = (me & 7) << 1
    low_half = ((me >> 3) & 1) == 0

    def slot_of(which):
        code = turns_of(which)
        low, high = code & 0xFFFF, code >> 16
        return 1 + ((jnp.where(low_half, low, high) >> at) & 3)

    slots = [slot_of(which) for which in range(3)]
    slot = jnp.where(two == 0, one * slots[0], jnp.where(one == 0, slots[1], slots[2]))
    core = [mask & 1 for mask in MASKS]
    theirs = (source & 1) ^ jnp.where(two == 0, one * core[0], jnp.where(one == 0, core[1], core[2]))
    steps = doubling_masks(n_blk)
    place = slot << len(steps)
    for step, mask in enumerate(steps):
        bit = (source >> (mask.bit_length() - 1)) & 1
        theirs = theirs ^ (bit * CROSSED)
        place = place | bit << step
    place = place | theirs << (len(steps) + 2)
    return (place << shift) | (ids & (rows - 1))


def absorb(state, logits, ids, start):
    top, total, picked = state
    new_top = jnp.maximum(top, jnp.max(logits, axis=0, keepdims=True))
    new_total = total * jnp.exp(top - new_top) + jnp.sum(
        jnp.exp(logits - new_top), axis=0, keepdims=True
    )
    chosen = []
    for k in range(0, ids.shape[0], 8):
        local = ids[k : k + 8] - start
        chunk, row = local >> 3, local & 7
        value = picked[k : k + 8]
        for c in range(logits.shape[0] // 8):
            found = jnp.take_along_axis(
                logits[c * 8 : c * 8 + 8], row, axis=0, mode="promise_in_bounds"
            )
            value = jnp.where(chunk == c, found, value)
        chosen.append(value)
    return (new_top, new_total, jnp.concatenate(chosen, axis=0))


def absorb_rows(state, refs, q_ref, ids, start):
    def one(state, rows, at):
        logits = SCALE * lax.dot_general(
            rows, q_ref[...], (((1,), (1,)), ((), ())), preferred_element_type=jnp.float32
        )
        return absorb(state, logits, ids, at)

    count = refs[0].shape[0]
    if count * len(refs) <= BLOCK:
        return one(state, jnp.concatenate([ref[...] for ref in refs], axis=0), start)

    for ref in refs:

        def step(index, state, ref=ref, start=start):
            at = pl.multiple_of(index * BLOCK, BLOCK)
            return one(state, ref[pl.ds(at, BLOCK)], start + at)

        state = lax.fori_loop(0, count // BLOCK, step, state)
        start = start + count
    return state


def empty(ids):
    wide = (1, ids.shape[1])
    return (
        jnp.full(wide, -jnp.inf, jnp.float32),
        jnp.zeros(wide, jnp.float32),
        jnp.zeros(ids.shape, jnp.float32),
    )


def first_kernel(rows, n_blk, q_ref, held_ref, ids_ref, local_ref, top_ref, total_ref, picked_ref):
    local = local_ids(ids_ref[...], rows, n_blk)
    local_ref[...] = local
    state = absorb_rows(empty(local), (held_ref,), q_ref, local, 0)
    top_ref[...], total_ref[...], picked_ref[...] = state


def next_kernel(start, n_pieces, q_ref, local_ref, top_ref, total_ref, picked_ref, *refs):
    pieces, outs = refs[:n_pieces], refs[n_pieces:]
    state = (top_ref[...], total_ref[...], picked_ref[...])
    state = absorb_rows(state, pieces, q_ref, local_ref[...], start)
    if len(outs) == 3:
        outs[0][...], outs[1][...], outs[2][...] = state
        return
    top, total, picked = state
    count = picked.shape[0]
    outs[0][:count] = picked
    outs[0][count:] = jnp.broadcast_to(top + jnp.log(total), (8, picked.shape[1]))


def last_kernel(mine_ref, other_ref, out_ref):
    count = out_ref.shape[0]
    mine, other = mine_ref[count : count + 1], other_ref[count : count + 1]
    top = jnp.maximum(mine, other)
    normalizer = top + jnp.log(jnp.exp(mine - top) + jnp.exp(other - top))
    out_ref[...] = mine_ref[:count] + other_ref[:count] - normalizer


def cost(n_rows, queries, ids):
    return pl.CostEstimate(
        flops=2 * n_rows * queries.shape[0] * queries.shape[1],
        bytes_accessed=2 * (queries.size + n_rows * queries.shape[1]) + 8 * ids.size,
        transcendentals=n_rows * queries.shape[0],
    )


PARAMS = pltpu.CompilerParams(vmem_limit_bytes=40 * 2**20)


def state_shapes(ids):
    wide = jax.ShapeDtypeStruct((1, ids.shape[1]), jnp.float32)
    return (wide, wide, jax.ShapeDtypeStruct(ids.shape, jnp.float32))


def first_call(rows, n_blk, queries, held, ids):
    return pl.pallas_call(
        functools.partial(first_kernel, rows, n_blk),
        out_shape=(jax.ShapeDtypeStruct(ids.shape, jnp.int32), *state_shapes(ids)),
        in_specs=[VMEM] * 3,
        out_specs=(VMEM,) * 4,
        compiler_params=PARAMS,
        cost_estimate=cost(held.shape[0], queries, ids),
    )(queries, held, ids)


def next_call(queries, pieces, start, local, state, last):
    part = jax.ShapeDtypeStruct((local.shape[0] + 8, local.shape[1]), jnp.float32)
    shapes = (part,) if last else state_shapes(local)
    return pl.pallas_call(
        functools.partial(next_kernel, start, len(pieces)),
        out_shape=shapes,
        in_specs=[VMEM] * (5 + len(pieces)),
        out_specs=(VMEM,) * len(shapes),
        compiler_params=PARAMS,
        cost_estimate=cost(len(pieces) * pieces[0].shape[0], queries, local),
    )(queries, local, *state, *pieces)


def last_call(mine, other, count):
    return pl.pallas_call(
        last_kernel,
        out_shape=jax.ShapeDtypeStruct((count, mine.shape[1]), jnp.float32),
        in_specs=[VMEM] * 2,
        out_specs=VMEM,
        compiler_params=PARAMS,
    )(mine, other)


def body(queries, passages, cand_ids):
    rows = passages.shape[0]
    n_blk = lax.axis_size("blk")
    n_all = 2 * n_blk
    held = passages
    for step, mask in enumerate(doubling_masks(n_blk)):
        got = lax.ppermute(held, AXES, [(i, i ^ mask) for i in range(n_all)])
        if step == 0:
            twice = lax.optimization_barrier(jnp.concatenate([held, held], axis=0))
            held = twice.at[rows:].set(got)
        else:
            held = jnp.concatenate([held, got], axis=0)
    far, near, last = (
        lax.ppermute(held, AXES, [(i, target(i, turn)) for i in range(n_all)])
        for turn in range(3)
    )
    count = held.shape[0]
    local, *state = first_call(rows, n_blk, queries, held, cand_ids.T)
    state = next_call(queries, [far], count, local, state, False)
    (mine,) = next_call(queries, [near, last], 2 * count, local, state, True)
    other = lax.ppermute(mine, "shard", [(0, 1), (1, 0)])
    return last_call(mine, other, cand_ids.shape[1]).T


def solution(mesh):
    return jax.shard_map(
        body,
        mesh=mesh,
        in_specs=(
            P(("groups", "blk"), None),
            P(("groups", "blk", "shard"), None),
            P(("groups", "blk"), None),
        ),
        out_specs=P(("groups", "blk"), None),
        check_vma=False,
    )
```

```python
import functools

import jax
import jax.numpy as jnp
from jax import lax
from jax.experimental import pallas as pl
from jax.experimental.pallas import tpu as pltpu
from jax.sharding import PartitionSpec as P

SCALE = 0.2
AXES = ("blk", "shard")
BLOCK = 256
VMEM = pl.BlockSpec(memory_space=pltpu.VMEM)


def parity(value):
    return value.bit_count() & 1


CROSSED = 0b11
MASKS = (2, 5, 7)
ORDERS = (
    (0, 2, 1),
    (1, 2, 0),
    (0, 2, 1),
    (1, 2, 0),
    (2, 1, 0),
    (0, 2, 1),
    (2, 1, 0),
    (0, 2, 1),
    (0, 2, 1),
    (1, 2, 0),
    (0, 2, 1),
    (1, 2, 0),
    (2, 1, 0),
    (0, 2, 1),
    (2, 1, 0),
    (0, 2, 1),
)


def doubling_bits(n_blk):
    return [2 << bit for bit in range(n_blk.bit_length() - 2, 1, -1)]


def crosses(number):
    return (CROSSED >> ((number >> 1) & 3)) & 1


def target(number, turn):
    return number ^ MASKS[ORDERS[number & 15][turn]]


def turns_of(which):
    code = 0
    for number in range(16):
        source = number ^ MASKS[which]
        code |= ORDERS[source].index(which) << (2 * number)
    return code


def local_ids(ids, rows, n_blk):
    me = lax.axis_index("blk") * 2 + lax.axis_index("shard")
    shift = rows.bit_length() - 1
    source = (ids >> shift) ^ me
    one, two = (source >> 1) & 1, (source >> 2) & 1
    at = (me & 7) << 1
    low_half = ((me >> 3) & 1) == 0

    def slot_of(which):
        code = turns_of(which)
        low, high = code & 0xFFFF, code >> 16
        return 1 + ((jnp.where(low_half, low, high) >> at) & 3)

    slots = [slot_of(which) for which in range(3)]
    slot = jnp.where(two == 0, one * slots[0], jnp.where(one == 0, slots[1], slots[2]))
    core = [mask & 1 for mask in MASKS]
    theirs = (source & 1) ^ jnp.where(two == 0, one * core[0], jnp.where(one == 0, core[1], core[2]))
    steps = doubling_bits(n_blk)
    place = slot << len(steps)
    cross = crosses(ids >> shift)
    for step, mask in enumerate(steps):
        bit = (source >> (mask.bit_length() - 1)) & 1
        theirs = theirs ^ (bit & cross)
        place = place | bit << step
    place = place | theirs << (len(steps) + 2)
    return (place << shift) | (ids & (rows - 1))


def absorb(state, logits, ids, start):
    top, total, picked = state
    new_top = jnp.maximum(top, jnp.max(logits, axis=0, keepdims=True))
    new_total = total * jnp.exp(top - new_top) + jnp.sum(
        jnp.exp(logits - new_top), axis=0, keepdims=True
    )
    chosen = []
    for k in range(0, ids.shape[0], 8):
        local = ids[k : k + 8] - start
        chunk, row = local >> 3, local & 7
        value = picked[k : k + 8]
        for c in range(logits.shape[0] // 8):
            found = jnp.take_along_axis(
                logits[c * 8 : c * 8 + 8], row, axis=0, mode="promise_in_bounds"
            )
            value = jnp.where(chunk == c, found, value)
        chosen.append(value)
    return (new_top, new_total, jnp.concatenate(chosen, axis=0))


def absorb_rows(state, refs, q_ref, ids, start):
    def one(state, rows, at):
        logits = SCALE * lax.dot_general(
            rows, q_ref[...], (((1,), (0,)), ((), ())), preferred_element_type=jnp.float32
        )
        return absorb(state, logits, ids, at)

    count = refs[0].shape[0]
    if count * len(refs) <= BLOCK:
        return one(state, jnp.concatenate([ref[...] for ref in refs], axis=0), start)

    for ref in refs:

        def step(index, state, ref=ref, start=start):
            at = pl.multiple_of(index * BLOCK, BLOCK)
            return one(state, ref[pl.ds(at, BLOCK)], start + at)

        state = lax.fori_loop(0, count // BLOCK, step, state)
        start = start + count
    return state


def empty(ids):
    wide = (1, ids.shape[1])
    return (
        jnp.full(wide, -jnp.inf, jnp.float32),
        jnp.zeros(wide, jnp.float32),
        jnp.zeros(ids.shape, jnp.float32),
    )


def first_kernel(rows, n_blk, q_ref, held_ref, ids_ref, local_ref, top_ref, total_ref, picked_ref):
    local = local_ids(ids_ref[...], rows, n_blk)
    local_ref[...] = local
    state = absorb_rows(empty(local), (held_ref,), q_ref, local, 0)
    top_ref[...], total_ref[...], picked_ref[...] = state


def next_kernel(start, n_pieces, q_ref, local_ref, top_ref, total_ref, picked_ref, *refs):
    pieces, outs = refs[:n_pieces], refs[n_pieces:]
    state = (top_ref[...], total_ref[...], picked_ref[...])
    state = absorb_rows(state, pieces, q_ref, local_ref[...], start)
    if len(outs) == 3:
        outs[0][...], outs[1][...], outs[2][...] = state
        return
    top, total, picked = state
    count = picked.shape[0]
    outs[0][:count] = picked
    outs[0][count:] = jnp.broadcast_to(top + jnp.log(total), (8, picked.shape[1]))


def last_kernel(mine_ref, other_ref, out_ref):
    count = out_ref.shape[0]
    mine, other = mine_ref[count : count + 1], other_ref[count : count + 1]
    top = jnp.maximum(mine, other)
    normalizer = top + jnp.log(jnp.exp(mine - top) + jnp.exp(other - top))
    out_ref[...] = mine_ref[:count] + other_ref[:count] - normalizer


def cost(n_rows, queries, ids):
    return pl.CostEstimate(
        flops=2 * n_rows * queries.size,
        bytes_accessed=2 * (queries.size + n_rows * queries.shape[0]) + 8 * ids.size,
        transcendentals=n_rows * queries.shape[1],
    )


PARAMS = pltpu.CompilerParams(vmem_limit_bytes=40 * 2**20)


def state_shapes(ids):
    wide = jax.ShapeDtypeStruct((1, ids.shape[1]), jnp.float32)
    return (wide, wide, jax.ShapeDtypeStruct(ids.shape, jnp.float32))


def first_call(rows, n_blk, queries, held, ids):
    return pl.pallas_call(
        functools.partial(first_kernel, rows, n_blk),
        out_shape=(jax.ShapeDtypeStruct(ids.shape, jnp.int32), *state_shapes(ids)),
        in_specs=[VMEM] * 3,
        out_specs=(VMEM,) * 4,
        compiler_params=PARAMS,
        cost_estimate=cost(held.shape[0], queries, ids),
    )(queries, held, ids)


def next_call(queries, pieces, start, local, state, last):
    part = jax.ShapeDtypeStruct((local.shape[0] + 8, local.shape[1]), jnp.float32)
    shapes = (part,) if last else state_shapes(local)
    return pl.pallas_call(
        functools.partial(next_kernel, start, len(pieces)),
        out_shape=shapes,
        in_specs=[VMEM] * (5 + len(pieces)),
        out_specs=(VMEM,) * len(shapes),
        compiler_params=PARAMS,
        cost_estimate=cost(len(pieces) * pieces[0].shape[0], queries, local),
    )(queries, local, *state, *pieces)


def last_call(mine, other, count):
    return pl.pallas_call(
        last_kernel,
        out_shape=jax.ShapeDtypeStruct((count, mine.shape[1]), jnp.float32),
        in_specs=[VMEM] * 2,
        out_specs=VMEM,
        compiler_params=PARAMS,
    )(mine, other)


def body(queries, passages, cand_ids):
    rows = passages.shape[0]
    n_blk = lax.axis_size("blk")
    n_all = 2 * n_blk
    queries = lax.optimization_barrier(queries.T)
    held = passages
    for step, mask in enumerate(doubling_bits(n_blk)):
        got = lax.ppermute(held, AXES, [(i, i ^ mask ^ crosses(i)) for i in range(n_all)])
        if step == 0:
            twice = lax.optimization_barrier(jnp.concatenate([held, held], axis=0))
            held = twice.at[rows:].set(got)
        else:
            held = jnp.concatenate([held, got], axis=0)
    far, near, last = (
        lax.ppermute(held, AXES, [(i, target(i, turn)) for i in range(n_all)])
        for turn in range(3)
    )
    count = held.shape[0]
    local, *state = first_call(rows, n_blk, queries, held, cand_ids.T)
    state = next_call(queries, [far], count, local, state, False)
    (mine,) = next_call(queries, [near, last], 2 * count, local, state, True)
    other = lax.ppermute(mine, "shard", [(0, 1), (1, 0)])
    return last_call(mine, other, cand_ids.shape[1]).T


def solution(mesh):
    return jax.shard_map(
        body,
        mesh=mesh,
        in_specs=(
            P(("groups", "blk"), None),
            P(("groups", "blk", "shard"), None),
            P(("groups", "blk"), None),
        ),
        out_specs=P(("groups", "blk"), None),
        check_vma=False,
    )
```

```python
import functools

import jax
import jax.numpy as jnp
from jax import lax
from jax.experimental import pallas as pl
from jax.experimental.pallas import tpu as pltpu
from jax.sharding import PartitionSpec as P

SCALE = 0.2
AXES = ("blk", "shard")
BLOCK = 256
VMEM = pl.BlockSpec(memory_space=pltpu.VMEM)


def parity(value):
    return value.bit_count() & 1


CROSSED = 0b10
SENDS = (
    (7, 2, 5),
    (5, 7, 2),
    (7, 2, 5),
    (5, 7, 2),
    (7, 5, 2),
    (7, 2, 5),
    (7, 5, 2),
    (7, 2, 5),
    (7, 2, 5),
    (5, 7, 2),
    (7, 2, 5),
    (5, 7, 2),
    (7, 5, 2),
    (7, 2, 5),
    (7, 5, 2),
    (7, 2, 5),
)


def doubling_bits(n_blk):
    return [2 << bit for bit in range(n_blk.bit_length() - 2, 1, -1)]


def crosses(number):
    return (CROSSED >> ((number >> 1) & 3)) & 1


def target(number, turn):
    return number ^ SENDS[number & 15][turn]


def receives(which):
    turns = cores = 0
    for number in range(16):
        for source in (number ^ (which << 1), number ^ (which << 1) ^ 1):
            for turn in range(3):
                if target(source, turn) == number:
                    turns |= turn << (2 * number)
                    cores |= ((source ^ number) & 1) << number
    return turns, cores


def local_ids(ids, rows, n_blk):
    me = lax.axis_index("blk") * 2 + lax.axis_index("shard")
    shift = rows.bit_length() - 1
    source = (ids >> shift) ^ me
    one, two = (source >> 1) & 1, (source >> 2) & 1
    here = me & 15

    def of_this(which):
        turns, cores = receives(which)
        turn = jnp.where(here < 8, turns & 0xFFFF, turns >> 16) >> ((here & 7) << 1)
        return 1 + (turn & 3), (cores >> here) & 1

    (slot_1, core_1), (slot_2, core_2), (slot_3, core_3) = [of_this(which) for which in (1, 2, 3)]

    def choose(own, first, second, third):
        return jnp.where(two == 0, jnp.where(one == 0, own, first), jnp.where(one == 0, second, third))

    slot = choose(0, slot_1, slot_2, slot_3)
    theirs = (source & 1) ^ choose(0, core_1, core_2, core_3)
    steps = doubling_bits(n_blk)
    place = slot << len(steps)
    cross = crosses(ids >> shift)
    for step, mask in enumerate(steps):
        bit = (source >> (mask.bit_length() - 1)) & 1
        theirs = theirs ^ (bit & cross)
        place = place | bit << step
    place = place | theirs << (len(steps) + 2)
    return (place << shift) | (ids & (rows - 1))


def absorb(state, logits, ids, start):
    top, total, picked = state
    new_top = jnp.maximum(top, jnp.max(logits, axis=0, keepdims=True))
    new_total = total * jnp.exp(top - new_top) + jnp.sum(
        jnp.exp(logits - new_top), axis=0, keepdims=True
    )
    chosen = []
    for k in range(0, ids.shape[0], 8):
        local = ids[k : k + 8] - start
        chunk, row = local >> 3, local & 7
        value = picked[k : k + 8]
        for c in range(logits.shape[0] // 8):
            found = jnp.take_along_axis(
                logits[c * 8 : c * 8 + 8], row, axis=0, mode="promise_in_bounds"
            )
            value = jnp.where(chunk == c, found, value)
        chosen.append(value)
    return (new_top, new_total, jnp.concatenate(chosen, axis=0))


def absorb_rows(state, refs, q_ref, ids, start):
    def one(state, rows, at):
        logits = SCALE * lax.dot_general(
            rows, q_ref[...], (((1,), (0,)), ((), ())), preferred_element_type=jnp.float32
        )
        return absorb(state, logits, ids, at)

    count = refs[0].shape[0]
    if count * len(refs) <= BLOCK:
        return one(state, jnp.concatenate([ref[...] for ref in refs], axis=0), start)

    for ref in refs:

        def step(index, state, ref=ref, start=start):
            at = pl.multiple_of(index * BLOCK, BLOCK)
            return one(state, ref[pl.ds(at, BLOCK)], start + at)

        state = lax.fori_loop(0, count // BLOCK, step, state)
        start = start + count
    return state


def empty(ids):
    wide = (1, ids.shape[1])
    return (
        jnp.full(wide, -jnp.inf, jnp.float32),
        jnp.zeros(wide, jnp.float32),
        jnp.zeros(ids.shape, jnp.float32),
    )


def first_kernel(rows, n_blk, q_ref, held_ref, ids_ref, local_ref, top_ref, total_ref, picked_ref):
    local = local_ids(ids_ref[...], rows, n_blk)
    local_ref[...] = local
    state = absorb_rows(empty(local), (held_ref,), q_ref, local, 0)
    top_ref[...], total_ref[...], picked_ref[...] = state


def next_kernel(start, n_pieces, q_ref, local_ref, top_ref, total_ref, picked_ref, *refs):
    pieces, outs = refs[:n_pieces], refs[n_pieces:]
    state = (top_ref[...], total_ref[...], picked_ref[...])
    state = absorb_rows(state, pieces, q_ref, local_ref[...], start)
    if len(outs) == 3:
        outs[0][...], outs[1][...], outs[2][...] = state
        return
    top, total, picked = state
    count = picked.shape[0]
    outs[0][:count] = picked
    outs[0][count:] = jnp.broadcast_to(top + jnp.log(total), (8, picked.shape[1]))


def last_kernel(mine_ref, other_ref, out_ref):
    count = out_ref.shape[0]
    mine, other = mine_ref[count : count + 1], other_ref[count : count + 1]
    top = jnp.maximum(mine, other)
    normalizer = top + jnp.log(jnp.exp(mine - top) + jnp.exp(other - top))
    out_ref[...] = mine_ref[:count] + other_ref[:count] - normalizer


def cost(n_rows, queries, ids):
    return pl.CostEstimate(
        flops=2 * n_rows * queries.size,
        bytes_accessed=2 * (queries.size + n_rows * queries.shape[0]) + 8 * ids.size,
        transcendentals=n_rows * queries.shape[1],
    )


PARAMS = pltpu.CompilerParams(vmem_limit_bytes=40 * 2**20)


def state_shapes(ids):
    wide = jax.ShapeDtypeStruct((1, ids.shape[1]), jnp.float32)
    return (wide, wide, jax.ShapeDtypeStruct(ids.shape, jnp.float32))


def first_call(rows, n_blk, queries, held, ids):
    return pl.pallas_call(
        functools.partial(first_kernel, rows, n_blk),
        out_shape=(jax.ShapeDtypeStruct(ids.shape, jnp.int32), *state_shapes(ids)),
        in_specs=[VMEM] * 3,
        out_specs=(VMEM,) * 4,
        compiler_params=PARAMS,
        cost_estimate=cost(held.shape[0], queries, ids),
    )(queries, held, ids)


def next_call(queries, pieces, start, local, state, last):
    part = jax.ShapeDtypeStruct((local.shape[0] + 8, local.shape[1]), jnp.float32)
    shapes = (part,) if last else state_shapes(local)
    return pl.pallas_call(
        functools.partial(next_kernel, start, len(pieces)),
        out_shape=shapes,
        in_specs=[VMEM] * (5 + len(pieces)),
        out_specs=(VMEM,) * len(shapes),
        compiler_params=PARAMS,
        cost_estimate=cost(len(pieces) * pieces[0].shape[0], queries, local),
    )(queries, local, *state, *pieces)


def last_call(mine, other, count):
    return pl.pallas_call(
        last_kernel,
        out_shape=jax.ShapeDtypeStruct((count, mine.shape[1]), jnp.float32),
        in_specs=[VMEM] * 2,
        out_specs=VMEM,
        compiler_params=PARAMS,
    )(mine, other)


def body(queries, passages, cand_ids):
    rows = passages.shape[0]
    n_blk = lax.axis_size("blk")
    n_all = 2 * n_blk
    queries = lax.optimization_barrier(queries.T)
    held = passages
    for step, mask in enumerate(doubling_bits(n_blk)):
        got = lax.ppermute(held, AXES, [(i, i ^ mask ^ crosses(i)) for i in range(n_all)])
        if step == 0:
            twice = lax.optimization_barrier(jnp.concatenate([held, held], axis=0))
            held = twice.at[rows:].set(got)
        else:
            held = jnp.concatenate([held, got], axis=0)
    far, near, last = (
        lax.ppermute(held, AXES, [(i, target(i, turn)) for i in range(n_all)])
        for turn in range(3)
    )
    count = held.shape[0]
    local, *state = first_call(rows, n_blk, queries, held, cand_ids.T)
    state = next_call(queries, [far], count, local, state, False)
    (mine,) = next_call(queries, [near, last], 2 * count, local, state, True)
    other = lax.ppermute(mine, "shard", [(0, 1), (1, 0)])
    return last_call(mine, other, cand_ids.shape[1]).T


def solution(mesh):
    return jax.shard_map(
        body,
        mesh=mesh,
        in_specs=(
            P(("groups", "blk"), None),
            P(("groups", "blk", "shard"), None),
            P(("groups", "blk"), None),
        ),
        out_specs=P(("groups", "blk"), None),
        check_vma=False,
    )
```
